32 devices in a mesh: groups: 2 (over x), tm: 16 (over z, y, core).
Axes of the slice: x: 2, y: 2, z: 4, core: 2. Of those that a mesh axis runs over, the one named last changes fastest.
Arguments:
- hidden: bfloat16 [1024, 512], P(('groups', 'tm')), parts along dimension 0, may hold values from -6 to 6
- durations: int32 [1024], P(('groups', 'tm')), parts along dimension 0, may hold values from 1 to 99, as said below
- mel_weight: bfloat16 [512, 80], replicated, may hold values from -0.25 to 0.25
- mel_bias: float32 [80], replicated, may hold values from -3 to 3
- pre_weight: bfloat16 [7, 80, 512], replicated, may hold values from -0.25 to 0.25
- pre_bias: float32 [512], replicated, may hold values from -3 to 3
- up_weight: bfloat16 [512, 16, 256], replicated, may hold values from -0.1875 to 0.1875
- up_bias: float32 [256], replicated, may hold values from -3 to 3
- res_weight: bfloat16 [4, 3, 256, 256], replicated, may hold values from -0.21875 to 0.21875
- res_bias: float32 [4, 256], replicated, may hold values from -3 to 3
Outputs:
- features: bfloat16 [262144, 256], P(('groups', 'tm')), parts along dimension 0
The draws below stay inside these ranges and needn't reach their ends.
There are 2 independent parts, one for each index of `groups`. The reference program is written for one: setup_inputs(seed, part) draws one part's arguments, and reference() takes and returns one part's arrays. A program takes and returns all parts, laid end to end along the dimension named above; an argument that names none is the same for every part. Nothing has to cross between parts.
Inputs may be any that keep to these rules, and one draw needn't show every extreme that they name: Every duration is 1 or more; the durations of the chapter sum to 16384; the phonemes of device j (rows j * 32 to (j + 1) * 32 - 1) span between 512 and 1536 frames, and the first frame of device j's phonemes lies within 256 of j * 1024, reached on some device in every draw, so that the frames of device j are covered only by phonemes of devices j - 1, j and j + 1.
All inputs are finite; a program needn't handle non-finite values.
Results may differ from the reference program's by a relative error of at most 0.01.
Values may be sent and summed in bfloat16 or wider, within the bound.
A program may use at most 128 MiB of HBM per device.

```python
import jax
import jax.numpy as jnp

D = 512
MEL = 80
CH = 512
UPCH = 256
KUP = 16
KPRE = 7
KRES = 3
PH_DEV = 32
FR_DEV = 1024
PHONEMES = 512
FRAMES = 16384
SAMPLES = 131072


def spread_levels(weights, extra):
    running = jnp.cumsum(weights, axis=1)
    whole = running[:, -1:]
    levels = running * extra[:, None] // whole
    before = jnp.concatenate([jnp.zeros((weights.shape[0], 1), jnp.int32), levels[:, :-1]], axis=1)
    return 1 + levels - before


def draw_durations(key, part):
    key = jax.random.fold_in(key, 11)
    key_drift, key_pick, key_weights = jax.random.split(key, 3)
    devices_count = PHONEMES // PH_DEV
    reach = FR_DEV // 4
    longest = 3 * FR_DEV // PH_DEV + 3
    drift = jax.random.randint(key_drift, (devices_count - 1,), -reach, reach + 1)
    pick = jax.random.randint(key_pick, (), 0, devices_count - 1)
    drift = jnp.where(jnp.arange(devices_count - 1) == pick, reach, drift).astype(jnp.int32)
    zero = jnp.zeros((1,), jnp.int32)
    edges = jnp.concatenate([zero, drift, zero])
    sums = (FR_DEV + edges[1:] - edges[:-1]).astype(jnp.int32)
    weights = jax.random.randint(key_weights, (devices_count, PH_DEV), 1, 3).astype(jnp.int32)
    drawn = spread_levels(weights, sums - PH_DEV)
    rest_extra = jnp.maximum(sums - longest - (PH_DEV - 1), 0).astype(jnp.int32)
    rest = spread_levels(weights[:, 1:], rest_extra)
    first = jnp.full((devices_count, 1), longest, jnp.int32)
    special = jnp.concatenate([first, rest], axis=1)
    chosen = (jnp.arange(devices_count) == pick)[:, None]
    spans = jnp.where(chosen, special, drawn)
    return spans.reshape(devices_count * PH_DEV).astype(jnp.int32)


def block_scale(key, shape, pieces, least, top_value):
    factor_of, own = 1.0, jax.random.fold_in(key, 6)
    for axis_at, parts in pieces:
        draws = jnp.exp(jax.random.uniform(jax.random.fold_in(own, axis_at), (parts,), jnp.float32, least / len(pieces), top_value / len(pieces)))
        factor_of = factor_of * jnp.repeat(draws, shape[axis_at] // parts).reshape([-1 if axis == axis_at else 1 for axis in range(len(shape))])
    return factor_of


def centred(stream_key, dims, deviation, bound, pieces=(), kind=jnp.bfloat16):
    level = block_scale(stream_key, dims, pieces, -0.22, 0.18) if pieces else 1.0
    entries = jax.random.normal(stream_key, dims, jnp.float32) * deviation * level
    return jnp.minimum(jnp.maximum(entries, -bound), bound).astype(kind)


def setup_inputs(seed: int = 0, part: int = 0) -> dict:
    splits = jax.random.split(jax.random.key(seed), 11)
    part_keys = jax.random.split(jax.random.fold_in(splits[10], part), 11)
    hidden = centred(part_keys[0], (PHONEMES, D), 1.0, 6.0, ((0, 16),))
    durations = draw_durations(jax.random.fold_in(jax.random.fold_in(splits[10], part), 71), part)
    mel_weight = centred(splits[2], (D, MEL), D ** -0.5, 0.25)
    mel_bias = centred(splits[3], (MEL,), 0.3, 3.0, (), jnp.float32)
    pre_weight = centred(splits[4], (KPRE, MEL, CH), (KPRE * MEL) ** -0.5, 0.25)
    pre_bias = centred(splits[5], (CH,), 0.3, 3.0, (), jnp.float32)
    up_weight = centred(splits[6], (CH, KUP, UPCH), (2 * CH) ** -0.5, 0.1875)
    up_bias = centred(splits[7], (UPCH,), 0.3, 3.0, (), jnp.float32)
    res_weight = centred(splits[8], (4, KRES, UPCH, UPCH), (KRES * UPCH) ** -0.5, 0.21875)
    res_bias = centred(splits[9], (4, UPCH), 0.3, 3.0, (), jnp.float32)
    return {"hidden": hidden, "durations": durations, "mel_weight": mel_weight, "mel_bias": mel_bias, "pre_weight": pre_weight, "pre_bias": pre_bias, "up_weight": up_weight, "up_bias": up_bias, "res_weight": res_weight, "res_bias": res_bias}


def leaky(v):
    return jnp.where(v >= 0, v, 0.1 * v)


def tap_sum(padded, weight, dilation, length):
    total = jnp.dot(padded[0:length], weight[0], preferred_element_type=jnp.float32)
    for k in range(1, weight.shape[0]):
        total = total + jnp.dot(padded[k * dilation:k * dilation + length], weight[k], preferred_element_type=jnp.float32)
    return total


def reference(hidden, durations, mel_weight, mel_bias, pre_weight, pre_bias, up_weight, up_bias, res_weight, res_bias):
    expanded = jnp.repeat(hidden, durations, axis=0, total_repeat_length=FRAMES)
    mel = (jnp.dot(expanded, mel_weight, preferred_element_type=jnp.float32) + mel_bias).astype(jnp.bfloat16)
    pre = tap_sum(jnp.pad(mel, ((3, 3), (0, 0))), pre_weight, 1, FRAMES) + pre_bias
    act = leaky(pre).astype(jnp.bfloat16)
    padded = jnp.pad(act, ((1, 1), (0, 0)))
    taps = jnp.dot(padded, up_weight.reshape(CH, KUP * UPCH), preferred_element_type=jnp.float32)
    taps = taps.reshape(FRAMES + 2, KUP, UPCH)
    lower = taps[1:FRAMES + 1, 4:8] + taps[0:FRAMES, 12:16]
    upper = taps[1:FRAMES + 1, 8:12] + taps[2:FRAMES + 2, 0:4]
    joined = jnp.concatenate([lower, upper], axis=1) + up_bias
    state = joined.reshape(SAMPLES, UPCH).astype(jnp.bfloat16)
    for pair, dilation in enumerate((1, 3)):
        inner = leaky(state.astype(jnp.float32)).astype(jnp.bfloat16)
        first = tap_sum(jnp.pad(inner, ((dilation, dilation), (0, 0))), res_weight[2 * pair], dilation, SAMPLES) + res_bias[2 * pair]
        first = leaky(first).astype(jnp.bfloat16)
        second = tap_sum(jnp.pad(first, ((1, 1), (0, 0))), res_weight[2 * pair + 1], 1, SAMPLES) + res_bias[2 * pair + 1]
        state = (state.astype(jnp.float32) + second).astype(jnp.bfloat16)
    return state
```

```python
import functools

import jax
import jax.numpy as jnp
from jax import lax
from jax.experimental import pallas as pl
from jax.experimental.pallas import tpu as pltpu
from jax.sharding import PartitionSpec as P

LANES = 128
TAPS = 16
PAD = 8
HALO = 16
MIB = 1024 * 1024


def leaky(v):
    return jnp.maximum(v, 0.1 * v)


def gather_kernel(
    count,
    dur_ref,
    hidden_ref,
    mel_w_ref,
    mel_b_ref,
    pre_w_hbm,
    up_w_hbm,
    mel_out,
    dur_out,
    pre_out,
    up_out,
    mel_own,
    mel_low,
    mel_high,
    dur_all,
    dur_own,
    pre_w,
    up_w,
    spread,
    load_sem,
    send_dur,
    recv_dur,
    send_mel,
    recv_mel,
):
    me = lax.axis_index("tm")
    load_pre = pltpu.make_async_copy(pre_w_hbm, pre_w, load_sem.at[0])
    load_up = pltpu.make_async_copy(up_w_hbm, up_w, load_sem.at[1])
    load_up.start()
    load_pre.start()
    barrier = pltpu.get_barrier_semaphore()
    for d in range(1, count):
        pl.semaphore_signal(
            barrier,
            inc=1,
            device_id={"tm": lax.rem(me + d, count)},
            device_id_type=pl.DeviceIdType.MESH,
        )
    phonemes = hidden_ref.shape[0]
    channels = mel_w_ref.shape[1]
    dur_own[...] = jnp.zeros_like(dur_own)
    dur_own[0:1, 0:phonemes] = dur_ref[...]
    mel = jnp.dot(hidden_ref[...], mel_w_ref[...], preferred_element_type=jnp.float32)
    mel = (mel + mel_b_ref[...]).astype(jnp.bfloat16)
    mel_own[...] = jnp.zeros_like(mel_own)
    mel_own[:, 0:channels] = mel
    pl.semaphore_wait(barrier, count - 1)

    copies = []
    for side, (hop, landing) in enumerate(((1, mel_low), (count - 1, mel_high))):
        copies.append(
            pltpu.make_async_remote_copy(
                src_ref=mel_own,
                dst_ref=landing,
                send_sem=send_mel.at[side],
                recv_sem=recv_mel.at[side],
                device_id={"tm": lax.rem(me + hop, count)},
                device_id_type=pl.DeviceIdType.MESH,
            )
        )
    for d in range(1, count):
        copies.append(
            pltpu.make_async_remote_copy(
                src_ref=dur_own,
                dst_ref=dur_all.at[d],
                send_sem=send_dur.at[d],
                recv_sem=recv_dur.at[d],
                device_id={"tm": lax.rem(me + d, count)},
                device_id_type=pl.DeviceIdType.MESH,
            )
        )
    for copy in copies:
        copy.start()

    load_pre.wait()
    pre_out[...] = jnp.zeros_like(pre_out)
    for k in range(pre_w.shape[0]):
        pre_out[k * LANES : k * LANES + channels, :] = pre_w[k]

    load_up.wait()
    step = 32
    width = up_w.shape[2]

    def relay(i, carry):
        first = pl.multiple_of(i * step, step)
        block = up_w[pl.ds(first, step)].reshape(step * TAPS, width).astype(jnp.float32)
        for h in range(width // LANES):
            spread[h] = block[:, h * LANES : (h + 1) * LANES]
        for k in range(TAPS):
            for h in range(width // LANES):
                part = spread[h, pl.ds(k, step, stride=TAPS), :]
                up_out[k, pl.ds(first, step), h * LANES : (h + 1) * LANES] = part.astype(jnp.bfloat16)
        return carry

    lax.fori_loop(0, up_w.shape[0] // step, relay, 0)

    for copy in copies:
        copy.wait()
    mel_out[...] = jnp.zeros_like(mel_out)
    mel_out[0:phonemes, :] = mel_low[...]
    mel_out[LANES : LANES + phonemes, :] = mel_own[...]
    mel_out[2 * LANES : 2 * LANES + phonemes, :] = mel_high[...]
    dur_out[0] = dur_own[...]
    for d in range(1, count):
        dur_out[d] = dur_all[d]


def main_kernel(
    count,
    frames,
    chunk,
    mel_ref,
    dur_ref,
    pre_w,
    pre_b,
    up_hbm,
    up_b,
    res_hbm,
    res_b,
    out_hbm,
    up_w,
    res_w,
    mel32,
    act32,
    x,
    xt,
    c,
    xt_sh,
    c_sh,
    weave,
    out_v,
    load_sem,
    out_sem,
):
    bf = jnp.bfloat16
    f32 = jnp.float32
    rows = frames + 2 * HALO
    me = lax.axis_index("tm")
    load_up = pltpu.make_async_copy(up_hbm, up_w, load_sem.at[0])
    load_res = pltpu.make_async_copy(res_hbm, res_w, load_sem.at[1])
    load_up.start()
    load_res.start()
    inside_low = me > 0
    inside_high = me < count - 1

    def edges(value, first):
        parts = []
        low, high = 0, value.shape[0]
        if first == 0:
            parts.append(jnp.where(inside_low, value[:HALO], 0.0))
            low = HALO
        if first + value.shape[0] == rows:
            high -= HALO
        parts.append(value[low:high])
        if first + value.shape[0] == rows:
            parts.append(jnp.where(inside_high, value[high:], 0.0))
        return jnp.concatenate(parts, axis=0) if len(parts) > 1 else value

    chunks = [(r, chunk) for r in range(0, rows, chunk)]

    durations = dur_ref[...].astype(f32)
    slot = lax.broadcasted_iota(jnp.int32, durations.shape, 0)
    lane_a = lax.broadcasted_iota(jnp.int32, (LANES, LANES), 0)
    lane_b = lax.broadcasted_iota(jnp.int32, (LANES, LANES), 1)
    before = jnp.where(lane_a < lane_b, 1.0, 0.0).astype(bf)
    earlier = jnp.sum(jnp.where((slot >= 1) & (slot <= me), durations, 0.0), axis=0)
    offset = jnp.sum(earlier, axis=(0, 1), keepdims=True)
    own = dur_ref[0].astype(f32)
    low = dur_ref[1].astype(f32)
    high = dur_ref[count - 1].astype(f32)
    total_own = jnp.sum(own, axis=(0, 1), keepdims=True)
    total_low = jnp.sum(low, axis=(0, 1), keepdims=True)
    bounds = []
    for tile, base, valid in (
        (low, offset - total_low, inside_low),
        (own, offset, None),
        (high, offset + total_own, inside_high),
    ):
        if valid is not None:
            tile = jnp.where(valid, tile, 0.0)
        start = (base + jnp.dot(tile.astype(bf), before, preferred_element_type=f32))[0:1]
        bounds.append((start, start + tile[0:1]))
    first_frame = me * frames - HALO
    for r, n in chunks:
        ids = (lax.broadcasted_iota(jnp.int32, (n, LANES), 0) + (first_frame + r)).astype(f32)
        hot = jnp.concatenate(
            [jnp.where((ids >= s) & (ids < e), 1.0, 0.0).astype(bf) for s, e in bounds], axis=1
        )
        mel32[PAD + r : PAD + r + n, :] = jnp.dot(hot, mel_ref[...], preferred_element_type=f32)

    for r, n in chunks:
        taps = jnp.concatenate(
            [mel32[PAD + r + k - 3 : PAD + r + k - 3 + n, :].astype(bf) for k in range(7)], axis=1
        )
        pre = jnp.dot(taps, pre_w[...], preferred_element_type=f32) + pre_b[...]
        act32[PAD + r : PAD + r + n, :] = edges(leaky(pre), r)

    def put_xt(value, p, r, n, dil):
        v = leaky(value.astype(f32))
        xt[p, r : r + n, :] = v.astype(bf)
        if p < dil:
            xt_sh[p, PAD + r : PAD + r + n, :] = edges(v, r)
        if p >= 8 - dil:
            xt_sh[p - 2, PAD + r : PAD + r + n, :] = edges(v, r)

    load_up.wait()
    for r, n in chunks:
        here = act32[PAD + r : PAD + r + n, :].astype(bf)
        prior = act32[PAD + r - 1 : PAD + r - 1 + n, :].astype(bf)
        after = act32[PAD + r + 1 : PAD + r + 1 + n, :].astype(bf)
        for p in range(8):
            other, tap = (prior, p + 12) if p < 4 else (after, p - 4)
            lhs = jnp.concatenate([here, other], axis=1)
            rhs = jnp.concatenate([up_w[p + 4], up_w[tap]], axis=0)
            value = (jnp.dot(lhs, rhs, preferred_element_type=f32) + up_b[...]).astype(bf)
            x[p, r : r + n, :] = value
            put_xt(value, p, r, n, 1)

    def gathered(main, shifted, index, p, dil, r, n):
        parts = []
        for k in (-1, 0, 1):
            q = p + k * dil
            if q < 0:
                parts.append(shifted[index(q + 8), PAD + r - 1 : PAD + r - 1 + n, :].astype(bf))
            elif q > 7:
                parts.append(shifted[index(q - 8), PAD + r + 1 : PAD + r + 1 + n, :].astype(bf))
            else:
                parts.append(main[q, r : r + n, :])
        return jnp.concatenate(parts, axis=1)

    def xt_index(q):
        return q if q < 3 else q - 2

    def c_index(q):
        return 0 if q == 0 else 1

    def weight(j):
        return res_w[j].reshape(3 * res_w.shape[2], res_w.shape[3])

    def inner(j, dil):
        for r, n in chunks:
            for p in range(8):
                lhs = gathered(xt, xt_sh, xt_index, p, dil, r, n)
                v = jnp.dot(lhs, weight(j), preferred_element_type=f32) + res_b[j : j + 1]
                v = leaky(v)
                c[p, r : r + n, :] = v.astype(bf)
                if p in (0, 7):
                    c_sh[c_index(p), PAD + r : PAD + r + n, :] = edges(v, r)

    load_res.wait()
    inner(0, 1)
    for r, n in chunks:
        for p in range(8):
            lhs = gathered(c, c_sh, c_index, p, 1, r, n)
            v = jnp.dot(lhs, weight(1), preferred_element_type=f32) + res_b[1:2]
            value = (x[p, r : r + n, :].astype(f32) + v).astype(bf)
            x[p, r : r + n, :] = value
            put_xt(value, p, r, n, 3)
    inner(2, 3)
    n = frames // 4
    stores = []
    for i in range(4):
        r = HALO + i * n
        for p in range(8):
            lhs = gathered(c, c_sh, c_index, p, 1, r, n)
            v = jnp.dot(lhs, weight(3), preferred_element_type=f32) + res_b[3:4]
            v = x[p, r : r + n, :].astype(f32) + v
            for h in range(2):
                weave[i % 2, h, pl.ds(p, n, stride=8), :] = v[:, h * LANES : (h + 1) * LANES]
        for h in range(2):
            out_v[i * n * 8 : (i + 1) * n * 8, h * LANES : (h + 1) * LANES] = weave[i % 2, h].astype(bf)
        store = pltpu.make_async_copy(
            out_v.at[pl.ds(i * n * 8, n * 8)], out_hbm.at[pl.ds(i * n * 8, n * 8)], out_sem.at[i]
        )
        store.start()
        stores.append(store)
    for store in stores:
        store.wait()


def on_device(
    frames,
    count,
    hidden,
    durations,
    mel_weight,
    mel_bias,
    pre_weight,
    pre_bias,
    up_weight,
    up_bias,
    res_weight,
    res_bias,
):
    phonemes, _ = hidden.shape
    taps, channels, inner = pre_weight.shape
    width = up_weight.shape[2]
    bf, f32, i32 = jnp.bfloat16, jnp.float32, jnp.int32
    vmem = pl.BlockSpec(memory_space=pltpu.VMEM)
    hbm = pl.BlockSpec(memory_space=pl.ANY)
    dma = pltpu.SemaphoreType.DMA
    mel_near, dur_all, pre_w, up_w = pl.pallas_call(
        functools.partial(gather_kernel, count),
        out_shape=(
            jax.ShapeDtypeStruct((3 * LANES, LANES), bf),
            jax.ShapeDtypeStruct((count, 8, LANES), i32),
            jax.ShapeDtypeStruct((taps * LANES, inner), bf),
            jax.ShapeDtypeStruct((TAPS, inner, width), bf),
        ),
        in_specs=[vmem, vmem, vmem, vmem, hbm, hbm],
        out_specs=(vmem, vmem, vmem, vmem),
        scratch_shapes=[
            pltpu.VMEM((phonemes, LANES), bf),
            pltpu.VMEM((phonemes, LANES), bf),
            pltpu.VMEM((phonemes, LANES), bf),
            pltpu.VMEM((count, 8, LANES), i32),
            pltpu.VMEM((8, LANES), i32),
            pltpu.VMEM(pre_weight.shape, bf),
            pltpu.VMEM(up_weight.shape, bf),
            pltpu.VMEM((2, 32 * TAPS, LANES), f32),
            dma((2,)),
            dma((count,)),
            dma((count,)),
            dma((2,)),
            dma((2,)),
        ],
        compiler_params=pltpu.CompilerParams(
            collective_id=0, has_side_effects=True, vmem_limit_bytes=24 * MIB
        ),
        name="gather_states",
    )(durations.reshape(1, -1), hidden, mel_weight, mel_bias.reshape(1, -1), pre_weight, up_weight)

    rows = frames + 2 * HALO
    chunk = rows // 3
    return pl.pallas_call(
        functools.partial(main_kernel, count, frames, chunk),
        out_shape=jax.ShapeDtypeStruct((frames * 8, width), bf),
        in_specs=[vmem, vmem, vmem, vmem, hbm, vmem, hbm, vmem],
        out_specs=hbm,
        scratch_shapes=[
            pltpu.VMEM(up_w.shape, bf),
            pltpu.VMEM(res_weight.shape, bf),
            pltpu.VMEM((rows + 2 * PAD, LANES), f32),
            pltpu.VMEM((rows + 2 * PAD, inner), f32),
            pltpu.VMEM((8, rows, width), bf),
            pltpu.VMEM((8, rows, width), bf),
            pltpu.VMEM((8, rows, width), bf),
            pltpu.VMEM((6, rows + 2 * PAD, width), f32),
            pltpu.VMEM((2, rows + 2 * PAD, width), f32),
            pltpu.VMEM((2, 2, frames * 2, LANES), f32),
            pltpu.VMEM((frames * 8, width), bf),
            dma((2,)),
            dma((4,)),
        ],
        compiler_params=pltpu.CompilerParams(vmem_limit_bytes=56 * MIB),
        name="vocoder_section",
    )(
        mel_near,
        dur_all,
        pre_w,
        pre_bias.reshape(1, -1),
        up_w,
        up_bias.reshape(1, -1),
        res_weight,
        res_bias,
    )


def solution(mesh):
    count = mesh.shape["tm"]

    def run(hidden, durations, *weights):
        frames = 32 * hidden.shape[0]
        return on_device(frames, count, hidden, durations, *weights)

    both = ("groups", "tm")
    in_specs = (P(both, None), P(both)) + (P(),) * 8
    return jax.shard_map(
        run, mesh=mesh, in_specs=in_specs, out_specs=P(both, None), check_vma=False
    )
```

```python
import functools

import jax
import jax.numpy as jnp
from jax import lax
from jax.experimental import pallas as pl
from jax.experimental.pallas import tpu as pltpu
from jax.sharding import PartitionSpec as P

LANES = 128
TAPS = 16
PAD = 8
HALO = 16
MIB = 1024 * 1024


def in_hbm(*arrays):
    return [pltpu.with_memory_space_constraint(a, pltpu.HBM) for a in arrays]


def leaky(v):
    return jnp.maximum(v, 0.1 * v)


def gather_kernel(
    count,
    dur_hbm,
    hidden_hbm,
    mel_w_hbm,
    mel_b_hbm,
    pre_w_hbm,
    up_w_hbm,
    mel_out,
    dur_out,
    pre_out,
    up_out,
    mel_own,
    mel_low,
    mel_high,
    dur_all,
    dur_own,
    pre_w,
    up_w,
    spread,
    dur_ref,
    hidden_ref,
    mel_w_ref,
    mel_b_ref,
    load_sem,
    send_dur,
    recv_dur,
    send_mel,
    recv_mel,
):
    me = lax.axis_index("tm")
    load_pre = pltpu.make_async_copy(pre_w_hbm, pre_w, load_sem.at[0])
    load_up = pltpu.make_async_copy(up_w_hbm, up_w, load_sem.at[1])
    first_loads = [
        pltpu.make_async_copy(source, target, load_sem.at[2 + i])
        for i, (source, target) in enumerate(
            (
                (dur_hbm, dur_ref),
                (hidden_hbm, hidden_ref),
                (mel_w_hbm, mel_w_ref),
                (mel_b_hbm, mel_b_ref),
            )
        )
    ]
    for load in first_loads:
        load.start()
    load_pre.start()
    load_up.start()
    barrier = pltpu.get_barrier_semaphore()
    for d in range(1, count):
        pl.semaphore_signal(
            barrier,
            inc=1,
            device_id={"tm": lax.rem(me + d, count)},
            device_id_type=pl.DeviceIdType.MESH,
        )
    phonemes = hidden_ref.shape[0]
    channels = mel_w_ref.shape[0]
    for load in first_loads:
        load.wait()
    dur_own[...] = jnp.zeros_like(dur_own)
    dur_own[0:1, 0:phonemes] = dur_ref[...]
    mel = lax.dot_general(
        hidden_ref[...],
        mel_w_ref[...],
        (((1,), (1,)), ((), ())),
        preferred_element_type=jnp.float32,
    )
    mel = (mel + mel_b_ref[...]).astype(jnp.bfloat16)
    mel_own[...] = jnp.zeros_like(mel_own)
    mel_own[:, 0:channels] = mel
    pl.semaphore_wait(barrier, count - 1)

    copies = []
    for side, (hop, landing) in enumerate(((1, mel_low), (count - 1, mel_high))):
        copies.append(
            pltpu.make_async_remote_copy(
                src_ref=mel_own,
                dst_ref=landing,
                send_sem=send_mel.at[side],
                recv_sem=recv_mel.at[side],
                device_id={"tm": lax.rem(me + hop, count)},
                device_id_type=pl.DeviceIdType.MESH,
            )
        )
    for d in range(1, count):
        copies.append(
            pltpu.make_async_remote_copy(
                src_ref=dur_own,
                dst_ref=dur_all.at[d],
                send_sem=send_dur.at[d],
                recv_sem=recv_dur.at[d],
                device_id={"tm": lax.rem(me + d, count)},
                device_id_type=pl.DeviceIdType.MESH,
            )
        )
    for copy in copies:
        copy.start()

    load_pre.wait()
    pre_out[...] = jnp.zeros_like(pre_out)
    for k in range(pre_w.shape[0]):
        pre_out[k * LANES : k * LANES + channels, :] = pre_w[k]

    load_up.wait()
    step = 32
    width = up_w.shape[2]

    def relay(i, carry):
        first = pl.multiple_of(i * step, step)
        block = up_w[pl.ds(first, step)].reshape(step * TAPS, width).astype(jnp.float32)
        for h in range(width // LANES):
            spread[h] = block[:, h * LANES : (h + 1) * LANES]
        for k in range(TAPS):
            for h in range(width // LANES):
                part = spread[h, pl.ds(k, step, stride=TAPS), :]
                up_out[k, pl.ds(first, step), h * LANES : (h + 1) * LANES] = part.astype(jnp.bfloat16)
        return carry

    lax.fori_loop(0, up_w.shape[0] // step, relay, 0)

    for copy in copies:
        copy.wait()
    mel_out[...] = jnp.zeros_like(mel_out)
    mel_out[0:phonemes, :] = mel_low[...]
    mel_out[LANES : LANES + phonemes, :] = mel_own[...]
    mel_out[2 * LANES : 2 * LANES + phonemes, :] = mel_high[...]
    dur_out[0] = dur_own[...]
    for d in range(1, count):
        dur_out[d] = dur_all[d]


def main_kernel(
    count,
    frames,
    chunk,
    mel_ref,
    dur_ref,
    pre_w,
    up_w,
    pre_b_hbm,
    up_b_hbm,
    res_hbm,
    res_b_hbm,
    out_hbm,
    pre_b,
    up_b,
    res_w,
    res_b,
    mel32,
    act32,
    x,
    xt,
    c,
    xt_sh,
    c_sh,
    weave,
    out_v,
    load_sem,
    out_sem,
):
    bf = jnp.bfloat16
    f32 = jnp.float32
    rows = frames + 2 * HALO
    me = lax.axis_index("tm")
    loads = [
        pltpu.make_async_copy(source, target, load_sem.at[i])
        for i, (source, target) in enumerate(
            ((pre_b_hbm, pre_b), (up_b_hbm, up_b), (res_b_hbm, res_b), (res_hbm, res_w))
        )
    ]
    for load in loads:
        load.start()
    inside_low = me > 0
    inside_high = me < count - 1

    def edges(value, first):
        parts = []
        low, high = 0, value.shape[0]
        if first == 0:
            parts.append(jnp.where(inside_low, value[:HALO], 0.0))
            low = HALO
        if first + value.shape[0] == rows:
            high -= HALO
        parts.append(value[low:high])
        if first + value.shape[0] == rows:
            parts.append(jnp.where(inside_high, value[high:], 0.0))
        return jnp.concatenate(parts, axis=0) if len(parts) > 1 else value

    chunks = [(r, chunk) for r in range(0, rows, chunk)]

    durations = dur_ref[...].astype(f32)
    slot = lax.broadcasted_iota(jnp.int32, durations.shape, 0)
    lane_a = lax.broadcasted_iota(jnp.int32, (LANES, LANES), 0)
    lane_b = lax.broadcasted_iota(jnp.int32, (LANES, LANES), 1)
    before = jnp.where(lane_a < lane_b, 1.0, 0.0).astype(bf)
    earlier = jnp.sum(jnp.where((slot >= 1) & (slot <= me), durations, 0.0), axis=0)
    offset = jnp.sum(earlier, axis=(0, 1), keepdims=True)
    own = dur_ref[0].astype(f32)
    low = dur_ref[1].astype(f32)
    high = dur_ref[count - 1].astype(f32)
    total_own = jnp.sum(own, axis=(0, 1), keepdims=True)
    total_low = jnp.sum(low, axis=(0, 1), keepdims=True)
    bounds = []
    for tile, base, valid in (
        (low, offset - total_low, inside_low),
        (own, offset, None),
        (high, offset + total_own, inside_high),
    ):
        if valid is not None:
            tile = jnp.where(valid, tile, 0.0)
        start = (base + jnp.dot(tile.astype(bf), before, preferred_element_type=f32))[0:1]
        bounds.append((start, start + tile[0:1]))
    first_frame = me * frames - HALO
    for r, n in chunks:
        ids = (lax.broadcasted_iota(jnp.int32, (n, LANES), 0) + (first_frame + r)).astype(f32)
        hot = jnp.concatenate(
            [jnp.where((ids >= s) & (ids < e), 1.0, 0.0).astype(bf) for s, e in bounds], axis=1
        )
        mel32[PAD + r : PAD + r + n, :] = jnp.dot(hot, mel_ref[...], preferred_element_type=f32)

    for load in loads[:3]:
        load.wait()
    for r, n in chunks:
        taps = jnp.concatenate(
            [mel32[PAD + r + k - 3 : PAD + r + k - 3 + n, :].astype(bf) for k in range(7)], axis=1
        )
        pre = jnp.dot(taps, pre_w[...], preferred_element_type=f32) + pre_b[...]
        act32[PAD + r : PAD + r + n, :] = edges(leaky(pre), r)

    def put_xt(value, p, r, n, dil):
        v = leaky(value.astype(f32))
        xt[p, r : r + n, :] = v.astype(bf)
        if p < dil:
            xt_sh[p, PAD + r : PAD + r + n, :] = edges(v, r)
        if p >= 8 - dil:
            xt_sh[p - 2, PAD + r : PAD + r + n, :] = edges(v, r)

    for r, n in chunks:
        here = act32[PAD + r : PAD + r + n, :].astype(bf)
        prior = act32[PAD + r - 1 : PAD + r - 1 + n, :].astype(bf)
        after = act32[PAD + r + 1 : PAD + r + 1 + n, :].astype(bf)
        for p in range(8):
            other, tap = (prior, p + 12) if p < 4 else (after, p - 4)
            lhs = jnp.concatenate([here, other], axis=1)
            rhs = jnp.concatenate([up_w[p + 4], up_w[tap]], axis=0)
            value = (jnp.dot(lhs, rhs, preferred_element_type=f32) + up_b[...]).astype(bf)
            x[p, r : r + n, :] = value
            put_xt(value, p, r, n, 1)

    def gathered(main, shifted, index, p, dil, r, n):
        parts = []
        for k in (-1, 0, 1):
            q = p + k * dil
            if q < 0:
                parts.append(shifted[index(q + 8), PAD + r - 1 : PAD + r - 1 + n, :].astype(bf))
            elif q > 7:
                parts.append(shifted[index(q - 8), PAD + r + 1 : PAD + r + 1 + n, :].astype(bf))
            else:
                parts.append(main[q, r : r + n, :])
        return jnp.concatenate(parts, axis=1)

    def xt_index(q):
        return q if q < 3 else q - 2

    def c_index(q):
        return 0 if q == 0 else 1

    def weight(j):
        return res_w[j].reshape(3 * res_w.shape[2], res_w.shape[3])

    def inner(j, dil):
        for r, n in chunks:
            for p in range(8):
                lhs = gathered(xt, xt_sh, xt_index, p, dil, r, n)
                v = jnp.dot(lhs, weight(j), preferred_element_type=f32) + res_b[j : j + 1]
                v = leaky(v)
                c[p, r : r + n, :] = v.astype(bf)
                if p in (0, 7):
                    c_sh[c_index(p), PAD + r : PAD + r + n, :] = edges(v, r)

    loads[3].wait()
    inner(0, 1)
    for r, n in chunks:
        for p in range(8):
            lhs = gathered(c, c_sh, c_index, p, 1, r, n)
            v = jnp.dot(lhs, weight(1), preferred_element_type=f32) + res_b[1:2]
            value = (x[p, r : r + n, :].astype(f32) + v).astype(bf)
            x[p, r : r + n, :] = value
            put_xt(value, p, r, n, 3)
    inner(2, 3)
    n = frames // 4
    stores = []
    for i in range(4):
        r = HALO + i * n
        for p in range(8):
            lhs = gathered(c, c_sh, c_index, p, 1, r, n)
            v = jnp.dot(lhs, weight(3), preferred_element_type=f32) + res_b[3:4]
            v = x[p, r : r + n, :].astype(f32) + v
            for h in range(2):
                weave[i % 2, h, pl.ds(p, n, stride=8), :] = v[:, h * LANES : (h + 1) * LANES]
        for h in range(2):
            out_v[i * n * 8 : (i + 1) * n * 8, h * LANES : (h + 1) * LANES] = weave[i % 2, h].astype(bf)
        store = pltpu.make_async_copy(
            out_v.at[pl.ds(i * n * 8, n * 8)], out_hbm.at[pl.ds(i * n * 8, n * 8)], out_sem.at[i]
        )
        store.start()
        stores.append(store)
    for store in stores:
        store.wait()


def on_device(
    frames,
    count,
    hidden,
    durations,
    mel_weight,
    mel_bias,
    pre_weight,
    pre_bias,
    up_weight,
    up_bias,
    res_weight,
    res_bias,
):
    phonemes, _ = hidden.shape
    taps, channels, inner = pre_weight.shape
    width = up_weight.shape[2]
    bf, f32, i32 = jnp.bfloat16, jnp.float32, jnp.int32
    vmem = pl.BlockSpec(memory_space=pltpu.VMEM)
    hbm = pl.BlockSpec(memory_space=pltpu.HBM)
    dma = pltpu.SemaphoreType.DMA
    mel_near, dur_all, pre_w, up_w = pl.pallas_call(
        functools.partial(gather_kernel, count),
        out_shape=(
            jax.ShapeDtypeStruct((3 * LANES, LANES), bf),
            jax.ShapeDtypeStruct((count, 8, LANES), i32),
            jax.ShapeDtypeStruct((taps * LANES, inner), bf),
            jax.ShapeDtypeStruct((TAPS, inner, width), bf),
        ),
        in_specs=[hbm] * 6,
        out_specs=(vmem, vmem, vmem, vmem),
        scratch_shapes=[
            pltpu.VMEM((phonemes, LANES), bf),
            pltpu.VMEM((phonemes, LANES), bf),
            pltpu.VMEM((phonemes, LANES), bf),
            pltpu.VMEM((count, 8, LANES), i32),
            pltpu.VMEM((8, LANES), i32),
            pltpu.VMEM(pre_weight.shape, bf),
            pltpu.VMEM(up_weight.shape, bf),
            pltpu.VMEM((2, 32 * TAPS, LANES), f32),
            pltpu.VMEM((1, phonemes), i32),
            pltpu.VMEM(hidden.shape, bf),
            pltpu.VMEM(mel_weight.shape[::-1], bf),
            pltpu.VMEM((1, channels), f32),
            dma((6,)),
            dma((count,)),
            dma((count,)),
            dma((2,)),
            dma((2,)),
        ],
        compiler_params=pltpu.CompilerParams(
            collective_id=0, has_side_effects=True, vmem_limit_bytes=24 * MIB
        ),
        name="gather_states",
    )(
        *in_hbm(
            durations.reshape(1, -1),
            hidden,
            mel_weight.T,
            mel_bias.reshape(1, -1),
            pre_weight,
            up_weight,
        )
    )

    rows = frames + 2 * HALO
    chunk = rows // 3
    return pl.pallas_call(
        functools.partial(main_kernel, count, frames, chunk),
        out_shape=jax.ShapeDtypeStruct((frames * 8, width), bf),
        in_specs=[vmem] * 4 + [hbm] * 4,
        out_specs=hbm,
        scratch_shapes=[
            pltpu.VMEM((1, inner), f32),
            pltpu.VMEM((1, width), f32),
            pltpu.VMEM(res_weight.shape, bf),
            pltpu.VMEM(res_bias.shape, f32),
            pltpu.VMEM((rows + 2 * PAD, LANES), f32),
            pltpu.VMEM((rows + 2 * PAD, inner), f32),
            pltpu.VMEM((8, rows, width), bf),
            pltpu.VMEM((8, rows, width), bf),
            pltpu.VMEM((8, rows, width), bf),
            pltpu.VMEM((6, rows + 2 * PAD, width), f32),
            pltpu.VMEM((2, rows + 2 * PAD, width), f32),
            pltpu.VMEM((2, 2, frames * 2, LANES), f32),
            pltpu.VMEM((frames * 8, width), bf),
            dma((4,)),
            dma((4,)),
        ],
        compiler_params=pltpu.CompilerParams(vmem_limit_bytes=44 * MIB),
        name="vocoder_section",
    )(
        mel_near,
        dur_all,
        pre_w,
        up_w,
        *in_hbm(pre_bias.reshape(1, -1), up_bias.reshape(1, -1), res_weight, res_bias),
    )


def solution(mesh):
    count = mesh.shape["tm"]

    def run(hidden, durations, *weights):
        frames = 32 * hidden.shape[0]
        return on_device(frames, count, hidden, durations, *weights)

    both = ("groups", "tm")
    in_specs = (P(both, None), P(both)) + (P(),) * 8
    return jax.shard_map(
        run, mesh=mesh, in_specs=in_specs, out_specs=P(both, None), check_vma=False
    )
```

```python
import functools

import jax
import jax.numpy as jnp
from jax import lax
from jax.experimental import pallas as pl
from jax.experimental.pallas import tpu as pltpu
from jax.sharding import PartitionSpec as P

LANES = 128
TAPS = 16
PAD = 8
HALO = 16
MIB = 1024 * 1024


def in_hbm(*arrays):
    return [pltpu.with_memory_space_constraint(a, pltpu.HBM) for a in arrays]


def leaky(v):
    return jnp.maximum(v, 0.1 * v)


def gather_kernel(
    count,
    dur_hbm,
    hidden_hbm,
    mel_w_hbm,
    mel_b_hbm,
    pre_w_hbm,
    up_w_hbm,
    mel_out,
    dur_out,
    pre_out,
    up_out,
    mel_own,
    mel_low,
    mel_high,
    dur_all,
    dur_own,
    pre_w,
    up_w,
    spread,
    dur_ref,
    hidden_ref,
    mel_w_ref,
    mel_b_ref,
    load_sem,
    send_dur,
    recv_dur,
    send_mel,
    recv_mel,
):
    me = lax.axis_index("tm")
    load_pre = pltpu.make_async_copy(pre_w_hbm, pre_w, load_sem.at[0])
    load_up = pltpu.make_async_copy(up_w_hbm, up_w, load_sem.at[1])
    first_loads = [
        pltpu.make_async_copy(source, target, load_sem.at[2 + i])
        for i, (source, target) in enumerate(
            (
                (dur_hbm, dur_ref),
                (hidden_hbm, hidden_ref),
                (mel_w_hbm, mel_w_ref),
                (mel_b_hbm, mel_b_ref),
            )
        )
    ]
    for load in first_loads:
        load.start()
    load_pre.start()
    load_up.start()
    barrier = pltpu.get_barrier_semaphore()
    for d in range(1, count):
        pl.semaphore_signal(
            barrier,
            inc=1,
            device_id={"tm": lax.rem(me + d, count)},
            device_id_type=pl.DeviceIdType.MESH,
        )
    phonemes = hidden_ref.shape[0]
    channels = mel_w_ref.shape[0]
    for load in first_loads:
        load.wait()
    dur_own[...] = jnp.zeros_like(dur_own)
    dur_own[0:1, 0:phonemes] = dur_ref[...]
    mel = lax.dot_general(
        hidden_ref[...],
        mel_w_ref[...],
        (((1,), (1,)), ((), ())),
        preferred_element_type=jnp.float32,
    )
    mel = (mel + mel_b_ref[...]).astype(jnp.bfloat16)
    mel_own[...] = jnp.zeros_like(mel_own)
    mel_own[:, 0:channels] = mel
    pl.semaphore_wait(barrier, count - 1)

    copies = []
    for side, (hop, landing) in enumerate(((1, mel_low), (count - 1, mel_high))):
        copies.append(
            pltpu.make_async_remote_copy(
                src_ref=mel_own,
                dst_ref=landing,
                send_sem=send_mel.at[side],
                recv_sem=recv_mel.at[side],
                device_id={"tm": lax.rem(me + hop, count)},
                device_id_type=pl.DeviceIdType.MESH,
            )
        )
    for d in range(1, count):
        copies.append(
            pltpu.make_async_remote_copy(
                src_ref=dur_own,
                dst_ref=dur_all.at[d],
                send_sem=send_dur.at[d],
                recv_sem=recv_dur.at[d],
                device_id={"tm": lax.rem(me + d, count)},
                device_id_type=pl.DeviceIdType.MESH,
            )
        )
    for copy in copies:
        copy.start()

    load_pre.wait()
    pre_out[...] = jnp.zeros_like(pre_out)
    for k in range(pre_w.shape[0]):
        pre_out[k * LANES : k * LANES + channels, :] = pre_w[k]

    load_up.wait()
    step = 32
    width = up_w.shape[2]

    def relay(i, carry):
        first = pl.multiple_of(i * step, step)
        block = up_w[pl.ds(first, step)].reshape(step * TAPS, width).astype(jnp.float32)
        for h in range(width // LANES):
            spread[h] = block[:, h * LANES : (h + 1) * LANES]
        for k in range(TAPS):
            for h in range(width // LANES):
                part = spread[h, pl.ds(k, step, stride=TAPS), :]
                up_out[k, pl.ds(first, step), h * LANES : (h + 1) * LANES] = part.astype(jnp.bfloat16)
        return carry

    lax.fori_loop(0, up_w.shape[0] // step, relay, 0)

    for copy in copies:
        copy.wait()
    mel_out[...] = jnp.zeros_like(mel_out)
    mel_out[0:phonemes, :] = mel_low[...]
    mel_out[LANES : LANES + phonemes, :] = mel_own[...]
    mel_out[2 * LANES : 2 * LANES + phonemes, :] = mel_high[...]
    dur_out[0] = dur_own[...]
    for d in range(1, count):
        dur_out[d] = dur_all[d]


def main_kernel(
    count,
    frames,
    chunk,
    mel_ref,
    dur_ref,
    pre_w,
    up_w,
    pre_b_hbm,
    up_b_hbm,
    res_hbm,
    res_b_hbm,
    out_hbm,
    pre_b,
    up_b,
    res_w,
    res_b,
    mel32,
    act32,
    x,
    xt,
    c,
    xt_sh,
    c_sh,
    weave,
    out_v,
    load_sem,
    out_sem,
):
    bf = jnp.bfloat16
    f32 = jnp.float32
    rows = frames + 2 * HALO
    me = lax.axis_index("tm")
    loads = [
        pltpu.make_async_copy(source, target, load_sem.at[i])
        for i, (source, target) in enumerate(
            ((pre_b_hbm, pre_b), (up_b_hbm, up_b), (res_b_hbm, res_b), (res_hbm, res_w))
        )
    ]
    for load in loads:
        load.start()
    inside_low = me > 0
    inside_high = me < count - 1

    def edges(value, first):
        parts = []
        low, high = 0, value.shape[0]
        if first == 0:
            parts.append(jnp.where(inside_low, value[:HALO], 0.0))
            low = HALO
        if first + value.shape[0] == rows:
            high -= HALO
        parts.append(value[low:high])
        if first + value.shape[0] == rows:
            parts.append(jnp.where(inside_high, value[high:], 0.0))
        return jnp.concatenate(parts, axis=0) if len(parts) > 1 else value

    chunks = [(r, chunk) for r in range(0, rows, chunk)]

    durations = dur_ref[...].astype(f32)
    slot = lax.broadcasted_iota(jnp.int32, durations.shape, 0)
    lane_a = lax.broadcasted_iota(jnp.int32, (LANES, LANES), 0)
    lane_b = lax.broadcasted_iota(jnp.int32, (LANES, LANES), 1)
    before = jnp.where(lane_a < lane_b, 1.0, 0.0).astype(bf)
    earlier = jnp.sum(jnp.where((slot >= 1) & (slot <= me), durations, 0.0), axis=0)
    offset = jnp.sum(earlier, axis=(0, 1), keepdims=True)
    own = dur_ref[0].astype(f32)
    low = dur_ref[1].astype(f32)
    high = dur_ref[count - 1].astype(f32)
    total_own = jnp.sum(own, axis=(0, 1), keepdims=True)
    total_low = jnp.sum(low, axis=(0, 1), keepdims=True)
    bounds = []
    for tile, base, valid in (
        (low, offset - total_low, inside_low),
        (own, offset, None),
        (high, offset + total_own, inside_high),
    ):
        if valid is not None:
            tile = jnp.where(valid, tile, 0.0)
        start = (base + jnp.dot(tile.astype(bf), before, preferred_element_type=f32))[0:1]
        bounds.append((start, start + tile[0:1]))
    first_frame = me * frames - HALO
    for r, n in chunks:
        ids = (lax.broadcasted_iota(jnp.int32, (n, LANES), 0) + (first_frame + r)).astype(f32)
        hot = jnp.concatenate(
            [jnp.where((ids >= s) & (ids < e), 1.0, 0.0).astype(bf) for s, e in bounds], axis=1
        )
        mel32[PAD + r : PAD + r + n, :] = jnp.dot(hot, mel_ref[...], preferred_element_type=f32)

    for load in loads[:3]:
        load.wait()
    for r, n in chunks:
        taps = jnp.concatenate(
            [mel32[PAD + r + k - 3 : PAD + r + k - 3 + n, :].astype(bf) for k in range(7)], axis=1
        )
        pre = jnp.dot(taps, pre_w[...], preferred_element_type=f32) + pre_b[...]
        act32[PAD + r : PAD + r + n, :] = edges(leaky(pre), r)

    def put_xt(value, p, r, n, dil):
        v = leaky(value.astype(f32))
        xt[p, r : r + n, :] = v.astype(bf)
        if p < dil:
            xt_sh[p, PAD + r : PAD + r + n, :] = edges(v, r)
        if p >= 8 - dil:
            xt_sh[p - 2, PAD + r : PAD + r + n, :] = edges(v, r)

    for r, n in chunks:
        here = act32[PAD + r : PAD + r + n, :].astype(bf)
        prior = act32[PAD + r - 1 : PAD + r - 1 + n, :].astype(bf)
        after = act32[PAD + r + 1 : PAD + r + 1 + n, :].astype(bf)
        for p in range(8):
            other, tap = (prior, p + 12) if p < 4 else (after, p - 4)
            lhs = jnp.concatenate([here, other], axis=1)
            rhs = jnp.concatenate([up_w[p + 4], up_w[tap]], axis=0)
            value = (jnp.dot(lhs, rhs, preferred_element_type=f32) + up_b[...]).astype(bf)
            x[p, r : r + n, :] = value
            put_xt(value, p, r, n, 1)

    def gathered(main, shifted, index, p, dil, r, n):
        parts = []
        for k in (-1, 0, 1):
            q = p + k * dil
            if q < 0:
                parts.append(shifted[index(q + 8), PAD + r - 1 : PAD + r - 1 + n, :].astype(bf))
            elif q > 7:
                parts.append(shifted[index(q - 8), PAD + r + 1 : PAD + r + 1 + n, :].astype(bf))
            else:
                parts.append(main[q, r : r + n, :])
        return jnp.concatenate(parts, axis=1)

    def xt_index(q):
        return q if q < 3 else q - 2

    def c_index(q):
        return 0 if q == 0 else 1

    def weight(j):
        return res_w[j].reshape(3 * res_w.shape[2], res_w.shape[3])

    def inner(j, dil):
        for r, n in chunks:
            for p in range(8):
                lhs = gathered(xt, xt_sh, xt_index, p, dil, r, n)
                v = jnp.dot(lhs, weight(j), preferred_element_type=f32) + res_b[j : j + 1]
                v = leaky(v)
                c[p, r : r + n, :] = v.astype(bf)
                if p in (0, 7):
                    c_sh[c_index(p), PAD + r : PAD + r + n, :] = edges(v, r)

    loads[3].wait()
    inner(0, 1)
    for r, n in chunks:
        for p in range(8):
            lhs = gathered(c, c_sh, c_index, p, 1, r, n)
            v = jnp.dot(lhs, weight(1), preferred_element_type=f32) + res_b[1:2]
            value = (x[p, r : r + n, :].astype(f32) + v).astype(bf)
            x[p, r : r + n, :] = value
            put_xt(value, p, r, n, 3)
    inner(2, 3)
    n = frames // 8
    stores = []
    for i in range(8):
        r = HALO + i * n
        for p in range(8):
            lhs = gathered(c, c_sh, c_index, p, 1, r, n)
            v = jnp.dot(lhs, weight(3), preferred_element_type=f32) + res_b[3:4]
            v = x[p, r : r + n, :].astype(f32) + v
            for h in range(2):
                weave[i % 2, h, pl.ds(p, n, stride=8), :] = v[:, h * LANES : (h + 1) * LANES]
        for h in range(2):
            out_v[i * n * 8 : (i + 1) * n * 8, h * LANES : (h + 1) * LANES] = weave[i % 2, h].astype(bf)
        store = pltpu.make_async_copy(
            out_v.at[pl.ds(i * n * 8, n * 8)], out_hbm.at[pl.ds(i * n * 8, n * 8)], out_sem.at[i]
        )
        store.start()
        stores.append(store)
    for store in stores:
        store.wait()


def on_device(
    frames,
    count,
    hidden,
    durations,
    mel_weight,
    mel_bias,
    pre_weight,
    pre_bias,
    up_weight,
    up_bias,
    res_weight,
    res_bias,
):
    phonemes, _ = hidden.shape
    taps, channels, inner = pre_weight.shape
    width = up_weight.shape[2]
    bf, f32, i32 = jnp.bfloat16, jnp.float32, jnp.int32
    vmem = pl.BlockSpec(memory_space=pltpu.VMEM)
    hbm = pl.BlockSpec(memory_space=pltpu.HBM)
    dma = pltpu.SemaphoreType.DMA
    mel_near, dur_all, pre_w, up_w = pl.pallas_call(
        functools.partial(gather_kernel, count),
        out_shape=(
            jax.ShapeDtypeStruct((3 * LANES, LANES), bf),
            jax.ShapeDtypeStruct((count, 8, LANES), i32),
            jax.ShapeDtypeStruct((taps * LANES, inner), bf),
            jax.ShapeDtypeStruct((TAPS, inner, width), bf),
        ),
        in_specs=[hbm] * 6,
        out_specs=(vmem, vmem, vmem, vmem),
        scratch_shapes=[
            pltpu.VMEM((phonemes, LANES), bf),
            pltpu.VMEM((phonemes, LANES), bf),
            pltpu.VMEM((phonemes, LANES), bf),
            pltpu.VMEM((count, 8, LANES), i32),
            pltpu.VMEM((8, LANES), i32),
            pltpu.VMEM(pre_weight.shape, bf),
            pltpu.VMEM(up_weight.shape, bf),
            pltpu.VMEM((2, 32 * TAPS, LANES), f32),
            pltpu.VMEM((1, phonemes), i32),
            pltpu.VMEM(hidden.shape, bf),
            pltpu.VMEM(mel_weight.shape[::-1], bf),
            pltpu.VMEM((1, channels), f32),
            dma((6,)),
            dma((count,)),
            dma((count,)),
            dma((2,)),
            dma((2,)),
        ],
        compiler_params=pltpu.CompilerParams(
            collective_id=0, has_side_effects=True, vmem_limit_bytes=24 * MIB
        ),
        name="gather_states",
    )(
        *in_hbm(
            durations.reshape(1, -1),
            hidden,
            mel_weight.T,
            mel_bias.reshape(1, -1),
            pre_weight,
            up_weight,
        )
    )

    rows = frames + 2 * HALO
    chunk = rows // 6
    return pl.pallas_call(
        functools.partial(main_kernel, count, frames, chunk),
        out_shape=jax.ShapeDtypeStruct((frames * 8, width), bf),
        in_specs=[vmem] * 4 + [hbm] * 4,
        out_specs=hbm,
        scratch_shapes=[
            pltpu.VMEM((1, inner), f32),
            pltpu.VMEM((1, width), f32),
            pltpu.VMEM(res_weight.shape, bf),
            pltpu.VMEM(res_bias.shape, f32),
            pltpu.VMEM((rows + 2 * PAD, LANES), f32),
            pltpu.VMEM((rows + 2 * PAD, inner), f32),
            pltpu.VMEM((8, rows, width), bf),
            pltpu.VMEM((8, rows, width), bf),
            pltpu.VMEM((8, rows, width), bf),
            pltpu.VMEM((6, rows + 2 * PAD, width), f32),
            pltpu.VMEM((2, rows + 2 * PAD, width), f32),
            pltpu.VMEM((2, 2, frames * 8 // 8, LANES), f32),
            pltpu.VMEM((frames * 8, width), bf),
            dma((4,)),
            dma((8,)),
        ],
        compiler_params=pltpu.CompilerParams(vmem_limit_bytes=44 * MIB),
        name="vocoder_section",
    )(
        mel_near,
        dur_all,
        pre_w,
        up_w,
        *in_hbm(pre_bias.reshape(1, -1), up_bias.reshape(1, -1), res_weight, res_bias),
    )


def solution(mesh):
    count = mesh.shape["tm"]

    def run(hidden, durations, *weights):
        frames = 32 * hidden.shape[0]
        return on_device(frames, count, hidden, durations, *weights)

    both = ("groups", "tm")
    in_specs = (P(both, None), P(both)) + (P(),) * 8
    return jax.shard_map(
        run, mesh=mesh, in_specs=in_specs, out_specs=P(both, None), check_vma=False
    )
```
